32 devices in a mesh: grp: 2 (over x), chi: 16 (over z, y, core).
Axes of the slice: x: 2, y: 2, z: 4, core: 2. Of those that a mesh axis runs over, the one named last changes fastest.
Arguments:
- edge: bfloat16 [768, 32, 384], P(('grp', 'chi')), parts along dimension 0, may hold values from -6 to 6
- proj_upper: bfloat16 [768, 32, 384], P(('grp', 'chi')), parts along dimension 0, may hold values from -0.3125 to 0.3125
- proj_lower: bfloat16 [768, 32, 384], P(('grp', 'chi')), parts along dimension 0, may hold values from -0.3125 to 0.3125
- site: bfloat16 [2048, 1024], P('grp'), parts along dimension 0, may hold values from -0.1875 to 0.1875
- chi_charge: int32 [768], P('grp'), parts along dimension 0, may hold values from 0 to 7
- bond_charge: int32 [64], P('grp'), parts along dimension 0, may hold values from 0 to 3
- new_charge: int32 [768], P('grp'), parts along dimension 0, may hold values from 0 to 10
Outputs:
- new_edge: bfloat16 [768, 32, 384], P(('grp', 'chi')), parts along dimension 0
The draws below stay inside these ranges and needn't reach their ends.
There are 2 independent parts, one for each index of `grp`. The reference program is written for one: setup_inputs(seed, part) draws one part's arguments, and reference() takes and returns one part's arrays. A program takes and returns all parts, laid end to end along the dimension named above; each array names one. Nothing has to cross between parts.
All inputs are finite; a program needn't handle non-finite values. Where the reference program divides by a largest or mean magnitude, that divisor is 1e-20 or more.
Results may differ from the reference program's by a relative error of at most 0.0059.
Values may be sent and summed in bfloat16 or wider, within the bound.
A program may use at most 320 MiB of HBM per device.

```python
import jax
import jax.numpy as jnp

CHI = 384
KBOND = 32


def with_ends(entries, own_key, smallest, largest):
    longest = entries.shape.index(max(entries.shape))
    spots = []
    for shift in (0, 1):
        where = [jax.random.randint(jax.random.fold_in(own_key, axis), (), 0, length) for axis, length in enumerate(entries.shape)]
        where[longest] = (where[longest] + shift) % entries.shape[longest]
        spots.append(tuple(where))
    return entries.at[spots[0]].set(smallest).at[spots[1]].set(largest)


def steps_of(key, extent, shards, smallest, top_value):
    loudness = 1.0
    for axis_at, parts in shards:
        heights = jax.random.uniform(jax.random.fold_in(jax.random.fold_in(key, 6), axis_at), (parts,), jnp.float32, smallest / len(shards), top_value / len(shards))
        loudness = loudness * jnp.repeat(jnp.exp(heights), extent[axis_at] // parts).reshape((-1,) + (1,) * (len(extent) - 1 - axis_at))
    return loudness


def noise(stream_key, dims, width, bound, cuts=(), kind=jnp.bfloat16):
    factor_of = steps_of(stream_key, dims, cuts, -0.22, 0.18) if cuts else 1.0
    result = jax.random.normal(stream_key, dims, jnp.float32) * width * factor_of
    return jnp.minimum(jnp.maximum(result, -bound), bound).astype(kind)


def setup_inputs(seed: int = 0, part: int = 0) -> dict:
    streams_of = jax.random.split(jax.random.key(seed), 8)
    own_keys = jax.random.split(jax.random.fold_in(streams_of[7], part), 8)
    edge = noise(own_keys[0], (CHI, KBOND, CHI), 1.0, 6.0, ((0, 16),))
    proj_upper = noise(own_keys[1], (CHI, KBOND, CHI), CHI ** -0.5, 0.3125, ((0, 16),))
    proj_lower = noise(own_keys[2], (CHI, KBOND, CHI), CHI ** -0.5, 0.3125, ((0, 16),))
    site = noise(own_keys[3], (KBOND * KBOND, KBOND * KBOND), (KBOND * KBOND) ** -0.5, 0.1875)
    chi_charge = with_ends(jax.random.randint(own_keys[4], (CHI,), 0, 8), jax.random.fold_in(own_keys[4], 1), 0, 7).astype(jnp.int32)
    bond_charge = with_ends(jax.random.randint(own_keys[5], (KBOND,), 0, 4), jax.random.fold_in(own_keys[5], 1), 0, 3).astype(jnp.int32)
    new_charge = with_ends(jax.random.randint(own_keys[6], (CHI,), 0, 11), jax.random.fold_in(own_keys[6], 1), 0, 10).astype(jnp.int32)
    return dict(edge=edge, proj_upper=proj_upper, proj_lower=proj_lower, site=site, chi_charge=chi_charge, bond_charge=bond_charge, new_charge=new_charge)


def reference(edge, proj_upper, proj_lower, site, chi_charge, bond_charge, new_charge):
    joined = chi_charge[:, None, None] + bond_charge[None, :, None]
    upper_mask = joined == new_charge[None, None, :]
    upper = jnp.where(upper_mask, proj_upper, jnp.zeros_like(proj_upper))
    lower = jnp.where(upper_mask, proj_lower, jnp.zeros_like(proj_lower))
    pair = (bond_charge[:, None] + bond_charge[None, :]).reshape(KBOND * KBOND)
    block = jnp.where(pair[:, None] == pair[None, :], site, jnp.zeros_like(site))
    half = jnp.dot(edge.reshape(CHI * KBOND, CHI), upper.reshape(CHI, KBOND * CHI),
                   preferred_element_type=jnp.float32).astype(jnp.bfloat16)
    half = half.reshape(CHI, KBOND, KBOND, CHI).transpose(0, 3, 1, 2).reshape(CHI * CHI, KBOND * KBOND)
    grown = jnp.dot(half, block, preferred_element_type=jnp.float32).astype(jnp.bfloat16)
    grown = grown.reshape(CHI, CHI, KBOND, KBOND).transpose(1, 2, 0, 3).reshape(CHI * KBOND, CHI * KBOND)
    raw = jnp.dot(grown, lower.reshape(CHI * KBOND, CHI), preferred_element_type=jnp.float32)
    raw = raw.reshape(CHI, KBOND, CHI)
    peak = jnp.max(jnp.abs(raw))
    return (raw / (peak + 1e-6)).astype(jnp.bfloat16)
```

```python
import functools

import jax
import jax.numpy as jnp
from jax import lax
from jax.experimental import pallas as pl
from jax.experimental.pallas import tpu as pltpu
from jax.sharding import PartitionSpec as P

BF = jnp.bfloat16
F32 = jnp.float32
EDGE, LOWER = 0, 1
RIGHT, LEFT, ACROSS, SIBLING = 0, 1, 2, 3
MESH = pl.DeviceIdType.MESH


def masked_rows(piece, charges, bond_charge, new_charge):
    keep = charges[:, None, None] + bond_charge[None, :, None] == new_charge[None, None, :]
    return jnp.where(keep, piece, jnp.zeros_like(piece))


def plain(edge, proj_upper, proj_lower, site, chi_charge, bond_charge, new_charge):
    rows = edge.shape[0]
    kdim = bond_charge.shape[0]
    width = chi_charge.shape[0]
    mine = lax.axis_index("chi") * rows
    pair = (bond_charge[:, None] + bond_charge[None, :]).reshape(kdim * kdim)
    block = jnp.where(pair[:, None] == pair[None, :], site, jnp.zeros_like(site))
    piece = lax.all_gather(proj_upper, "chi", axis=0, tiled=True)
    count = piece.shape[0]
    masked = masked_rows(piece, chi_charge, bond_charge, new_charge)
    half = jnp.dot(
        edge.reshape(rows * kdim, count),
        masked.reshape(count, kdim * width),
        preferred_element_type=F32,
    )
    half = half.astype(BF).reshape(rows, kdim * kdim, width)
    grown = jnp.einsum("bxc,xy->byc", half, block, preferred_element_type=F32).astype(BF)
    grown = grown.reshape(rows, kdim, kdim, width)
    own_charges = lax.dynamic_slice_in_dim(chi_charge, mine, rows)
    lower = masked_rows(proj_lower, own_charges, bond_charge, new_charge)
    raw = lax.psum_scatter(
        jnp.einsum("brdc,bde->cre", grown, lower, preferred_element_type=F32),
        "chi",
        scatter_dimension=0,
        tiled=True,
    )
    largest = lax.pmax(jnp.max(jnp.abs(raw)), "chi")
    return (raw / (largest + 1e-06)).astype(BF)


def kernel(
    n, depth, edge_ref, lower_ref, upper_ref, block_ref, out_ref,
    edge_all, lower_all, swap, up_rx, up_wide, up_t, state, total, peaks,
    swap_send, swap_recv, up_send, up_recv, blk_send, blk_recv, peak_send, peak_recv,
):
    kdim, rows, width = edge_ref.shape
    part = kdim // 2
    wide = 2 * rows
    chips = n // 2
    pairs = kdim * kdim
    me = lax.axis_index("chi")
    core = lax.rem(me, 2)
    chip = me // 2
    y = lax.rem(chip, 2)
    z = chip // 2
    sibling = me + 1 - 2 * core

    barrier = pltpu.get_barrier_semaphore()

    def greet(j, carry):
        pl.semaphore_signal(barrier, inc=1, device_id={"chi": lax.rem(me + j, n)}, device_id_type=MESH)
        return carry

    lax.fori_loop(1, n, greet, 0)
    pl.semaphore_wait(barrier, n - 1)

    ins = (edge_ref, lower_ref)
    fulls = (edge_all, lower_all)

    def swap_copy(which):
        return pltpu.make_async_remote_copy(
            src_ref=ins[which].at[pl.ds(part * (1 - core), part)],
            dst_ref=swap.at[which],
            send_sem=swap_send.at[which],
            recv_sem=swap_recv.at[which],
            device_id={"chi": sibling},
            device_id_type=MESH,
        )

    def block_copy(which, q, side, way, target):
        here = fulls[which].at[q, pl.ds(part * side, part)]
        return pltpu.make_async_remote_copy(
            src_ref=here,
            dst_ref=here,
            send_sem=blk_send.at[which, q, way],
            recv_sem=blk_recv.at[which, q, side],
            device_id={"chi": target},
            device_id_type=MESH,
        )

    def ways(which, q):
        targets = (me + 4, me - 4, me + 2 - 4 * y, sibling)

        def send(way):
            block_copy(which, q, core, way, targets[way]).start()

        def leave(way):
            block_copy(which, q, core, way, targets[way]).wait_send()

        return send, leave

    def arrived(which, q, side):
        block_copy(which, q, side, SIBLING, sibling).wait_recv()

    def up_copy(j):
        to = lax.rem(me + j, n)
        return pltpu.make_async_remote_copy(
            src_ref=upper_ref.at[to],
            dst_ref=up_rx.at[me],
            send_sem=up_send.at[j],
            recv_sem=up_recv.at[j],
            device_id={"chi": to},
            device_id_type=MESH,
        )

    def each(lo, hi, act):
        def body(j, carry):
            act(j)
            return carry

        lax.fori_loop(lo, hi, body, 0)

    def join(which):
        swap_copy(which).wait_recv()

        def body(j):
            own = ins[which][part * core + j].astype(F32)
            other = swap[which, j].astype(F32)
            first = jnp.where(core == 0, own, other)
            second = jnp.where(core == 0, other, own)
            fulls[which][chip, part * core + j] = jnp.concatenate([first, second], axis=0).astype(BF)

        each(0, part, body)

    def open_ring(which):
        send, _ = ways(which, chip)
        pl.when(z < depth - 1)(lambda: send(RIGHT))
        pl.when(z > 0)(lambda: send(LEFT))
        send(ACROSS)
        send(SIBLING)

    def along(which, s):
        @pl.when(z - s >= 0)
        def _():
            q = chip - 2 * s
            arrived(which, q, core)
            send, _ = ways(which, q)
            pl.when(z < depth - 1)(lambda: send(RIGHT))
            send(ACROSS)
            send(SIBLING)

        @pl.when(z + s < depth)
        def _():
            q = chip + 2 * s
            arrived(which, q, core)
            send, _ = ways(which, q)
            pl.when(z > 0)(lambda: send(LEFT))
            send(ACROSS)
            send(SIBLING)

    def beside(which, s):
        other = chip + 1 - 2 * y
        for sign in (-1, 1) if s else (1,):
            @pl.when(jnp.logical_and(z + sign * s >= 0, z + sign * s < depth))
            def _():
                q = other + 2 * sign * s
                arrived(which, q, core)
                block_copy(which, q, core, SIBLING, sibling).start()

    def close_ring(which):
        each(0, chips, lambda q: arrived(which, q, 1 - core))

    def sent(which):
        def body(q):
            _, leave = ways(which, q)
            column = q // 2
            mine = lax.rem(q, 2) == y
            pl.when(jnp.logical_and(mine, jnp.logical_and(column <= z, z < depth - 1)))(lambda: leave(RIGHT))
            pl.when(jnp.logical_and(mine, jnp.logical_and(column >= z, z > 0)))(lambda: leave(LEFT))
            pl.when(mine)(lambda: leave(ACROSS))
            leave(SIBLING)

        each(0, chips, body)

    swap_copy(EDGE).start()
    swap_copy(LOWER).start()
    join(EDGE)
    open_ring(EDGE)
    each(1, n, lambda j: up_copy(j).start())
    join(LOWER)
    up_rx[me] = upper_ref[me]
    along(EDGE, 1)
    beside(EDGE, 0)
    each(1, n, lambda j: up_copy(j).wait_recv())
    for j in range(n):
        up_wide[j * rows:(j + 1) * rows, :] = up_rx[j].astype(F32)
    up_t[...] = up_wide[...].T.astype(BF)
    along(EDGE, 2)
    beside(EDGE, 1)
    along(EDGE, 3)
    open_ring(LOWER)
    beside(EDGE, 2)
    beside(EDGE, 3)
    close_ring(EDGE)

    def first(j):
        right = edge_all[:, j].reshape(width, width)
        half = lax.dot_general(up_t[...], right, (((1,), (1,)), ((), ())), preferred_element_type=F32)
        at = pl.multiple_of(j * kdim, kdim)
        state[1:rows + 1, pl.ds(at, kdim), :] = half.astype(BF).reshape(rows, kdim, width)

    each(0, kdim, first)

    def second(j):
        c = 2 * j
        right = jnp.concatenate([state[c + 1], state[c + 2]], axis=1)
        grown = jnp.dot(block_ref[...], right, preferred_element_type=F32).astype(BF)
        state[c] = grown[:, :width]
        state[c + 1] = grown[:, width:]

    third_of = rows // 6
    along(LOWER, 1)
    beside(LOWER, 0)
    each(0, third_of, second)
    along(LOWER, 2)
    beside(LOWER, 1)
    each(third_of, 2 * third_of, second)
    along(LOWER, 3)
    beside(LOWER, 2)
    each(2 * third_of, rows // 2, second)
    beside(LOWER, 3)
    close_ring(LOWER)

    total[...] = jnp.zeros_like(total)

    def third(j):
        at = pl.multiple_of(2 * j * kdim, 2 * kdim)
        left = jnp.concatenate(
            [
                state[0:rows, pl.ds(at, kdim), :].reshape(rows * kdim, width),
                state[0:rows, pl.ds(at + kdim, kdim), :].reshape(rows * kdim, width),
            ],
            axis=1,
        )
        right = jnp.concatenate(
            [lower_all[:, 2 * j].reshape(width, width), lower_all[:, 2 * j + 1].reshape(width, width)], axis=0
        )
        total[...] += jnp.dot(left, right, preferred_element_type=F32)

    each(0, kdim // 2, third)

    peaks[me] = jnp.full(peaks.shape[1:], jnp.max(jnp.abs(total[...])), F32)

    def peak_copy(j):
        return pltpu.make_async_remote_copy(
            src_ref=peaks.at[me],
            dst_ref=peaks.at[me],
            send_sem=peak_send.at[j],
            recv_sem=peak_recv.at[j],
            device_id={"chi": lax.rem(me + j, n)},
            device_id_type=MESH,
        )

    each(1, n, lambda j: peak_copy(j).start())
    each(0, 2, lambda w: pltpu.make_async_remote_copy(
        src_ref=edge_ref.at[pl.ds(0, part)], dst_ref=swap.at[w], send_sem=swap_send.at[w],
        recv_sem=swap_recv.at[w], device_id={"chi": sibling}, device_id_type=MESH).wait_send())
    each(1, n, lambda j: up_copy(j).wait_send())
    sent(EDGE)
    sent(LOWER)
    each(1, n, lambda j: peak_copy(j).wait_recv())
    each(1, n, lambda j: peak_copy(j).wait_send())
    largest = jnp.max(peaks[...])
    out_ref[...] = (total[...] / (largest + 1e-06)).astype(BF)


def fused(n, edge, proj_upper, proj_lower, site, chi_charge, bond_charge, new_charge):
    rows, kdim, width = edge.shape
    mine = lax.axis_index("chi") * rows
    own_charges = lax.dynamic_slice_in_dim(chi_charge, mine, rows)
    upper = masked_rows(proj_upper, own_charges, bond_charge, new_charge)
    lower = masked_rows(proj_lower, own_charges, bond_charge, new_charge)
    upper = upper.reshape(rows, kdim, n, rows).transpose(2, 0, 3, 1).reshape(n, rows, rows * kdim)
    pair = (bond_charge[:, None] + bond_charge[None, :]).reshape(kdim * kdim)
    block = jnp.where(pair[:, None] == pair[None, :], site, jnp.zeros_like(site))
    block = block.reshape(kdim * kdim, kdim, kdim).transpose(2, 1, 0).reshape(kdim * kdim, kdim * kdim)
    chips = n // 2
    part = kdim // 2
    dma = pltpu.SemaphoreType.DMA
    vmem = pl.BlockSpec(memory_space=pltpu.VMEM)
    out = pl.pallas_call(
        functools.partial(kernel, n, chips // 2),
        out_shape=jax.ShapeDtypeStruct((rows * kdim, width), BF),
        in_specs=[vmem] * 4,
        out_specs=vmem,
        scratch_shapes=[
            pltpu.VMEM((chips, kdim, 2 * rows, width), BF),
            pltpu.VMEM((chips, kdim, 2 * rows, width), BF),
            pltpu.VMEM((2, part, rows, width), BF),
            pltpu.VMEM((n, rows, rows * kdim), BF),
            pltpu.VMEM((width, rows * kdim), F32),
            pltpu.VMEM((rows * kdim, width), BF),
            pltpu.VMEM((rows + 1, kdim * kdim, width), BF),
            pltpu.VMEM((rows * kdim, width), F32),
            pltpu.VMEM((n, 8, 128), F32),
            dma((2,)), dma((2,)),
            dma((n,)), dma((n,)),
            dma((2, chips, 4)), dma((2, chips, 2)),
            dma((n,)), dma((n,)),
        ],
        compiler_params=pltpu.CompilerParams(
            collective_id=0, has_side_effects=True, vmem_limit_bytes=63 * 1024 * 1024
        ),
        name="edge_update",
    )(edge.transpose(1, 0, 2), lower.transpose(1, 0, 2), upper, block)
    return out.reshape(rows, kdim, width)


def solution(mesh):
    n = mesh.shape["chi"]

    def local(edge, *rest):
        rows, kdim, width = edge.shape
        if n == 16 and rows % 8 == 0 and rows % 6 == 0 and kdim % 32 == 0 and width % 128 == 0:
            return fused(n, edge, *rest)
        return plain(edge, *rest)

    placed = (
        P(("grp", "chi"), None, None),
        P(("grp", "chi"), None, None),
        P(("grp", "chi"), None, None),
        P("grp", None),
        P("grp"),
        P("grp"),
        P("grp"),
    )
    return jax.shard_map(
        local, mesh=mesh, in_specs=placed, out_specs=P(("grp", "chi"), None, None), check_vma=False
    )
```

```python
import functools

import jax
import jax.numpy as jnp
from jax import lax
from jax.experimental import pallas as pl
from jax.experimental.pallas import tpu as pltpu
from jax.sharding import PartitionSpec as P

BF = jnp.bfloat16
F32 = jnp.float32
LANES = 128
GROUP = 4
CUTS = 2
EDGE, LOWER = 0, 1
RIGHT, LEFT, ACROSS, SIBLING = 0, 1, 2, 3
MESH = pl.DeviceIdType.MESH


def masked_rows(piece, charges, bond_charge, new_charge):
    keep = charges[:, None, None] + bond_charge[None, :, None] == new_charge[None, None, :]
    return jnp.where(keep, piece, jnp.zeros_like(piece))


def plain(edge, proj_upper, proj_lower, site, chi_charge, bond_charge, new_charge):
    rows = edge.shape[0]
    kdim = bond_charge.shape[0]
    width = chi_charge.shape[0]
    mine = lax.axis_index("chi") * rows
    pair = (bond_charge[:, None] + bond_charge[None, :]).reshape(kdim * kdim)
    block = jnp.where(pair[:, None] == pair[None, :], site, jnp.zeros_like(site))
    piece = lax.all_gather(proj_upper, "chi", axis=0, tiled=True)
    count = piece.shape[0]
    masked = masked_rows(piece, chi_charge, bond_charge, new_charge)
    half = jnp.dot(
        edge.reshape(rows * kdim, count),
        masked.reshape(count, kdim * width),
        preferred_element_type=F32,
    )
    half = half.astype(BF).reshape(rows, kdim * kdim, width)
    grown = jnp.einsum("bxc,xy->byc", half, block, preferred_element_type=F32).astype(BF)
    grown = grown.reshape(rows, kdim, kdim, width)
    own_charges = lax.dynamic_slice_in_dim(chi_charge, mine, rows)
    lower = masked_rows(proj_lower, own_charges, bond_charge, new_charge)
    raw = lax.psum_scatter(
        jnp.einsum("brdc,bde->cre", grown, lower, preferred_element_type=F32),
        "chi",
        scatter_dimension=0,
        tiled=True,
    )
    largest = lax.pmax(jnp.max(jnp.abs(raw)), "chi")
    return (raw / (largest + 1e-06)).astype(BF)


def kernel(
    n, depth, edge_ref, lower_ref, upper_ref, block_ref, own_ref, chip_ref, new_ref, bond_ref, out_ref,
    edge_all, lower_all, swap, up_tx, up_rx, up_wide, up_t, state, total, peaks,
    swap_send, swap_recv, up_send, up_recv, blk_send, blk_recv, peak_send, peak_recv,
):
    kdim, rows, width = edge_ref.shape
    part = kdim // 2
    wide = 2 * rows
    chips = n // 2
    pairs = kdim * kdim
    me = lax.axis_index("chi")
    core = lax.rem(me, 2)
    chip = me // 2
    y = lax.rem(chip, 2)
    z = chip // 2
    sibling = me + 1 - 2 * core

    barrier = pltpu.get_barrier_semaphore()

    def greet(j, carry):
        pl.semaphore_signal(barrier, inc=1, device_id={"chi": lax.rem(me + j, n)}, device_id_type=MESH)
        return carry

    lax.fori_loop(1, n, greet, 0)
    pl.semaphore_wait(barrier, n - 1)

    ins = (edge_ref, lower_ref)
    fulls = (edge_all, lower_all)

    def swap_copy(which):
        return pltpu.make_async_remote_copy(
            src_ref=ins[which].at[pl.ds(part * (1 - core), part)],
            dst_ref=swap.at[which],
            send_sem=swap_send.at[which],
            recv_sem=swap_recv.at[which],
            device_id={"chi": sibling},
            device_id_type=MESH,
        )

    def slot_of(q, at):
        qz, az = q // 2, at // 2
        gap = jnp.abs(qz - az)
        rank = jnp.int32(0)
        for other in range(depth):
            far = jnp.abs(other - az)
            nearer = jnp.logical_or(far < gap, jnp.logical_and(far == gap, other < qz))
            rank = rank + nearer.astype(jnp.int32)
        return 2 * rank + lax.rem(q + at, 2)

    piece = part // CUTS

    def block_copy(which, q, side, way, target, cut):
        here, there = slot_of(q, chip), slot_of(q, target // 2)
        return pltpu.make_async_remote_copy(
            src_ref=fulls[which].at[here, pl.ds(part * side + piece * cut, piece)],
            dst_ref=fulls[which].at[there, pl.ds(part * side + piece * cut, piece)],
            send_sem=blk_send.at[which, q, way, cut],
            recv_sem=blk_recv.at[which, there, side, cut],
            device_id={"chi": target},
            device_id_type=MESH,
        )

    def ways(which, q, cut):
        targets = (me + 4, me - 4, me + 2 - 4 * y, sibling)

        def send(way):
            block_copy(which, q, core, way, targets[way], cut).start()

        def leave(way):
            block_copy(which, q, core, way, targets[way], cut).wait_send()

        return send, leave

    def arrived(which, q, side, cut):
        block_copy(which, q, side, SIBLING, sibling, cut).wait_recv()

    def whole(which, lo, hi):
        def wait(slot):
            for cut in range(CUTS):
                here = fulls[which].at[slot, pl.ds(part * (1 - core) + piece * cut, piece)]
                pltpu.make_async_remote_copy(
                    src_ref=here, dst_ref=here, send_sem=blk_send.at[which, 0, SIBLING, cut],
                    recv_sem=blk_recv.at[which, slot, 1 - core, cut],
                    device_id={"chi": sibling}, device_id_type=MESH,
                ).wait_recv()

        each(lo, hi, wait)

    def up_copy(j):
        to = lax.rem(me + j, n)
        return pltpu.make_async_remote_copy(
            src_ref=up_tx.at[to],
            dst_ref=up_rx.at[me],
            send_sem=up_send.at[j],
            recv_sem=up_recv.at[j],
            device_id={"chi": to},
            device_id_type=MESH,
        )

    def each(lo, hi, act):
        def body(j, carry):
            act(j)
            return carry

        lax.fori_loop(lo, hi, body, 0)

    def join(which):
        swap_copy(which).wait_recv()

        def body(j):
            own = ins[which][part * core + j].astype(F32)
            other = swap[which, j].astype(F32)
            first = jnp.where(core == 0, own, other)
            second = jnp.where(core == 0, other, own)
            both = jnp.concatenate([first, second], axis=0)
            if which == LOWER:
                keep = chip_ref[...] + bond_ref[part * core + j] == new_ref[...]
                both = jnp.where(keep, both, jnp.zeros_like(both))
            fulls[which][0, part * core + j] = both.astype(BF)

        each(0, part, body)

    beyond = chip + 1 - 2 * y

    def open_across(which):
        for cut in range(CUTS):
            send, _ = ways(which, chip, cut)
            send(ACROSS)
            send(SIBLING)

    def open_line(which):
        for cut in range(CUTS):
            send, _ = ways(which, chip, cut)
            pl.when(z < depth - 1)(lambda: send(RIGHT))
            pl.when(z > 0)(lambda: send(LEFT))

    def along(which, s):
        for cut in range(CUTS):
            @pl.when(z - s >= 0)
            def _():
                q = chip - 2 * s
                arrived(which, q, core, cut)
                send, _ = ways(which, q, cut)
                pl.when(z < depth - 1)(lambda: send(RIGHT))
                send(ACROSS)
                send(SIBLING)

            @pl.when(z + s < depth)
            def _():
                q = chip + 2 * s
                arrived(which, q, core, cut)
                send, _ = ways(which, q, cut)
                pl.when(z > 0)(lambda: send(LEFT))
                send(ACROSS)
                send(SIBLING)

    def beside(which, s):
        for cut in range(CUTS):
            for sign in (-1, 1) if s else (1,):
                @pl.when(jnp.logical_and(z + sign * s >= 0, z + sign * s < depth))
                def _():
                    q = beyond + 2 * sign * s
                    arrived(which, q, core, cut)
                    block_copy(which, q, core, SIBLING, sibling, cut).start()

    def sent(which):
        def body(q):
            column = q // 2
            mine = lax.rem(q, 2) == y
            for cut in range(CUTS):
                _, leave = ways(which, q, cut)
                pl.when(jnp.logical_and(mine, jnp.logical_and(column <= z, z < depth - 1)))(lambda: leave(RIGHT))
                pl.when(jnp.logical_and(mine, jnp.logical_and(column >= z, z > 0)))(lambda: leave(LEFT))
                pl.when(mine)(lambda: leave(ACROSS))
                leave(SIBLING)

        each(0, chips, body)

    def rows_of(full, t, j):
        lo, hi = LANES * t, LANES * (t + 1)
        cuts = []
        for slot in range(lo // wide, (hi + wide - 1) // wide):
            start, stop = max(lo - slot * wide, 0), min(hi - slot * wide, wide)
            cuts.append(full[slot, j, start:stop, :])
        return cuts

    def first(t, lo, hi):
        def body(j):
            right = jnp.concatenate(rows_of(edge_all, t, 2 * j) + rows_of(edge_all, t, 2 * j + 1), axis=0)
            half = lax.dot_general(up_t[...], right, (((1,), (1,)), ((), ())), preferred_element_type=F32)
            half = half.astype(BF)
            at = pl.multiple_of(2 * j * kdim, 2 * kdim)
            state[t, 1:rows + 1, pl.ds(at, kdim), :] = half[:, :LANES].reshape(rows, kdim, LANES)
            state[t, 1:rows + 1, pl.ds(at + kdim, kdim), :] = half[:, LANES:].reshape(rows, kdim, LANES)

        each(lo, hi, body)

    def second(t, lo, hi):
        def body(j):
            c = GROUP * j
            right = jnp.concatenate([state[t, c + 1 + i] for i in range(GROUP)], axis=1)
            grown = jnp.dot(block_ref[...], right, preferred_element_type=F32).astype(BF)
            for i in range(GROUP):
                state[t, c + i] = grown[:, i * LANES:(i + 1) * LANES]

        each(lo, hi, body)

    def third(t):
        def body(j):
            lefts, rights = [], []
            for i in range(4):
                at = pl.multiple_of((4 * j + i) * kdim, kdim)
                lefts.append(state[t, 0:rows, pl.ds(at, kdim), :].reshape(rows * kdim, LANES))
                rights += rows_of(lower_all, t, 4 * j + i)
            total[...] += jnp.dot(
                jnp.concatenate(lefts, axis=1), jnp.concatenate(rights, axis=0), preferred_element_type=F32
            )

        each(0, kdim // 4, body)

    steps = rows // GROUP
    swap_copy(EDGE).start()
    swap_copy(LOWER).start()
    join(EDGE)
    open_line(EDGE)
    open_across(EDGE)
    upper = jnp.where(own_ref[...] == new_ref[...], upper_ref[...].astype(F32), 0.0).T
    for j in range(n):
        up_tx[j] = upper[j * rows:(j + 1) * rows, :].astype(BF)
    each(1, n, lambda j: up_copy(j).start())
    join(LOWER)
    up_rx[me] = up_tx[me]
    total[...] = jnp.zeros_like(total)
    beside(EDGE, 0)
    along(EDGE, 1)
    each(1, n, lambda j: up_copy(j).wait_recv())
    up_wide[...] = up_rx[...].astype(F32)
    lane = lax.broadcasted_iota(jnp.int32, (n, width), 1)
    sender = lax.broadcasted_iota(jnp.int32, (n, width), 0)
    spread = jnp.logical_and(lane >= sender * rows, lane < (sender + 1) * rows).astype(F32).astype(BF)
    within = lax.rem(lax.broadcasted_iota(jnp.int32, (rows, 1, width), 2), rows)
    chosen = within == lax.broadcasted_iota(jnp.int32, (rows, 1, width), 0)
    for c in range(rows):
        spots = lax.dot_general(
            up_wide[:, c, :].astype(BF), spread, (((0,), (0,)), ((), ())), preferred_element_type=F32
        ).reshape(rows, kdim, width)
        up_t[c * kdim:(c + 1) * kdim, :] = jnp.sum(jnp.where(chosen, spots, 0.0), axis=0).astype(BF)
    beside(EDGE, 1)
    along(EDGE, 2)
    whole(EDGE, 0, 3)
    first(0, 0, kdim // 2)
    beside(EDGE, 2)
    along(EDGE, 3)
    open_line(LOWER)
    open_across(LOWER)
    second(0, 0, steps)
    beside(EDGE, 3)
    whole(EDGE, 3, 6)
    first(1, 0, kdim // 2)
    beside(LOWER, 0)
    along(LOWER, 1)
    whole(EDGE, 6, chips)
    first(2, 0, kdim // 2)
    second(1, 0, steps // 2)
    beside(LOWER, 1)
    along(LOWER, 2)
    second(1, steps // 2, steps)
    second(2, 0, steps // 2)
    beside(LOWER, 2)
    along(LOWER, 3)
    second(2, steps // 2, steps)
    whole(LOWER, 0, 3)
    third(0)
    whole(LOWER, 3, 6)
    third(1)
    beside(LOWER, 3)
    whole(LOWER, 6, chips)
    third(2)

    peaks[me] = jnp.full(peaks.shape[1:], jnp.max(jnp.abs(total[...])), F32)

    def peak_copy(j):
        return pltpu.make_async_remote_copy(
            src_ref=peaks.at[me],
            dst_ref=peaks.at[me],
            send_sem=peak_send.at[j],
            recv_sem=peak_recv.at[j],
            device_id={"chi": lax.rem(me + j, n)},
            device_id_type=MESH,
        )

    each(1, n, lambda j: peak_copy(j).start())
    each(0, 2, lambda w: pltpu.make_async_remote_copy(
        src_ref=edge_ref.at[pl.ds(0, part)], dst_ref=swap.at[w], send_sem=swap_send.at[w],
        recv_sem=swap_recv.at[w], device_id={"chi": sibling}, device_id_type=MESH).wait_send())
    each(1, n, lambda j: up_copy(j).wait_send())
    sent(EDGE)
    sent(LOWER)
    each(1, n, lambda j: peak_copy(j).wait_recv())
    each(1, n, lambda j: peak_copy(j).wait_send())
    largest = jnp.max(peaks[...])
    out_ref[...] = (total[...] / (largest + 1e-06)).astype(BF)


def fused(n, edge, proj_upper, proj_lower, site, chi_charge, bond_charge, new_charge):
    rows, kdim, width = edge.shape
    mine = lax.axis_index("chi") * rows
    own = lax.dynamic_slice_in_dim(chi_charge, mine, rows)
    own = (own[:, None] + bond_charge[None, :]).reshape(rows * kdim, 1)
    start = lax.axis_index("chi") // 2 * (2 * rows)
    chip = lax.dynamic_slice_in_dim(chi_charge, start, 2 * rows)[:, None]
    pair = (bond_charge[:, None] + bond_charge[None, :]).reshape(kdim * kdim)
    block = jnp.where(pair[:, None] == pair[None, :], site, jnp.zeros_like(site))
    block = block.reshape(kdim * kdim, kdim, kdim).transpose(2, 1, 0).reshape(kdim * kdim, kdim * kdim)
    chips = n // 2
    part = kdim // 2
    dma = pltpu.SemaphoreType.DMA
    vmem = pl.BlockSpec(memory_space=pltpu.VMEM)
    out = pl.pallas_call(
        functools.partial(kernel, n, chips // 2),
        out_shape=jax.ShapeDtypeStruct((rows * kdim, width), BF),
        in_specs=[vmem] * 7 + [pl.BlockSpec(memory_space=pltpu.SMEM)],
        out_specs=vmem,
        scratch_shapes=[
            pltpu.VMEM((chips, kdim, 2 * rows, width), BF),
            pltpu.VMEM((chips, kdim, 2 * rows, width), BF),
            pltpu.VMEM((2, part, rows, width), BF),
            pltpu.VMEM((n, rows, rows * kdim), BF),
            pltpu.VMEM((n, rows, rows * kdim), BF),
            pltpu.VMEM((n, rows, rows * kdim), F32),
            pltpu.VMEM((rows * kdim, width), BF),
            pltpu.VMEM((width // LANES, rows + 1, kdim * kdim, LANES), BF),
            pltpu.VMEM((rows * kdim, width), F32),
            pltpu.VMEM((n, 8, 128), F32),
            dma((2,)), dma((2,)),
            dma((n,)), dma((n,)),
            dma((2, chips, 4, CUTS)), dma((2, chips, 2, CUTS)),
            dma((n,)), dma((n,)),
        ],
        compiler_params=pltpu.CompilerParams(
            collective_id=0, has_side_effects=True, vmem_limit_bytes=63 * 1024 * 1024
        ),
        name="edge_update",
    )(
        edge.transpose(1, 0, 2), proj_lower.transpose(1, 0, 2), proj_upper.reshape(rows * kdim, width), block,
        own, chip, new_charge[None, :], bond_charge,
    )
    return out.reshape(rows, kdim, width)


def solution(mesh):
    n = mesh.shape["chi"]

    def local(edge, *rest):
        rows, kdim, width = edge.shape
        if n == 16 and rows % 8 == 0 and rows % 6 == 0 and kdim % 32 == 0 and width == 3 * LANES:
            return fused(n, edge, *rest)
        return plain(edge, *rest)

    placed = (
        P(("grp", "chi"), None, None),
        P(("grp", "chi"), None, None),
        P(("grp", "chi"), None, None),
        P("grp", None),
        P("grp"),
        P("grp"),
        P("grp"),
    )
    return jax.shard_map(
        local, mesh=mesh, in_specs=placed, out_specs=P(("grp", "chi"), None, None), check_vma=False
    )
```

```python
import functools

import jax
import jax.numpy as jnp
from jax import lax
from jax.experimental import pallas as pl
from jax.experimental.pallas import tpu as pltpu
from jax.sharding import PartitionSpec as P

BF = jnp.bfloat16
F32 = jnp.float32
LANES = 128
GROUP = 4
CUTS = 2
EDGE, LOWER = 0, 1
RIGHT, LEFT, ACROSS, SIBLING = 0, 1, 2, 3
MESH = pl.DeviceIdType.MESH


def masked_rows(piece, charges, bond_charge, new_charge):
    keep = charges[:, None, None] + bond_charge[None, :, None] == new_charge[None, None, :]
    return jnp.where(keep, piece, jnp.zeros_like(piece))


def plain(edge, proj_upper, proj_lower, site, chi_charge, bond_charge, new_charge):
    rows = edge.shape[0]
    kdim = bond_charge.shape[0]
    width = chi_charge.shape[0]
    mine = lax.axis_index("chi") * rows
    pair = (bond_charge[:, None] + bond_charge[None, :]).reshape(kdim * kdim)
    block = jnp.where(pair[:, None] == pair[None, :], site, jnp.zeros_like(site))
    piece = lax.all_gather(proj_upper, "chi", axis=0, tiled=True)
    count = piece.shape[0]
    masked = masked_rows(piece, chi_charge, bond_charge, new_charge)
    half = jnp.dot(
        edge.reshape(rows * kdim, count),
        masked.reshape(count, kdim * width),
        preferred_element_type=F32,
    )
    half = half.astype(BF).reshape(rows, kdim * kdim, width)
    grown = jnp.einsum("bxc,xy->byc", half, block, preferred_element_type=F32).astype(BF)
    grown = grown.reshape(rows, kdim, kdim, width)
    own_charges = lax.dynamic_slice_in_dim(chi_charge, mine, rows)
    lower = masked_rows(proj_lower, own_charges, bond_charge, new_charge)
    raw = lax.psum_scatter(
        jnp.einsum("brdc,bde->cre", grown, lower, preferred_element_type=F32),
        "chi",
        scatter_dimension=0,
        tiled=True,
    )
    largest = lax.pmax(jnp.max(jnp.abs(raw)), "chi")
    return (raw / (largest + 1e-06)).astype(BF)


def kernel(
    n, depth, edge_ref, lower_ref, upper_ref, site_ref, own_ref, chip_ref, new_ref, pair_ref, column_ref, bond_ref, out_ref,
    edge_all, lower_all, swap, up_tx, up_rx, up_wide, up_t, turned, block_ref, state, total, peaks,
    swap_send, swap_recv, up_send, up_recv, blk_send, blk_recv, peak_send, peak_recv,
):
    kdim, rows, width = edge_ref.shape
    part = kdim // 2
    wide = 2 * rows
    chips = n // 2
    pairs = kdim * kdim
    me = lax.axis_index("chi")
    core = lax.rem(me, 2)
    chip = me // 2
    y = lax.rem(chip, 2)
    z = chip // 2
    sibling = me + 1 - 2 * core

    barrier = pltpu.get_barrier_semaphore()

    def greet(j, carry):
        pl.semaphore_signal(barrier, inc=1, device_id={"chi": lax.rem(me + j, n)}, device_id_type=MESH)
        return carry

    lax.fori_loop(1, n, greet, 0)
    pl.semaphore_wait(barrier, n - 1)

    ins = (edge_ref, lower_ref)
    fulls = (edge_all, lower_all)

    def swap_copy(which):
        return pltpu.make_async_remote_copy(
            src_ref=ins[which].at[pl.ds(part * (1 - core), part)],
            dst_ref=swap.at[which],
            send_sem=swap_send.at[which],
            recv_sem=swap_recv.at[which],
            device_id={"chi": sibling},
            device_id_type=MESH,
        )

    def slot_of(q, at):
        qz, az = q // 2, at // 2
        gap = jnp.abs(qz - az)
        rank = jnp.int32(0)
        for other in range(depth):
            far = jnp.abs(other - az)
            nearer = jnp.logical_or(far < gap, jnp.logical_and(far == gap, other < qz))
            rank = rank + nearer.astype(jnp.int32)
        return 2 * rank + lax.rem(q + at, 2)

    piece = part // CUTS

    def block_copy(which, q, side, way, target, cut):
        here, there = slot_of(q, chip), slot_of(q, target // 2)
        return pltpu.make_async_remote_copy(
            src_ref=fulls[which].at[here, pl.ds(part * side + piece * cut, piece)],
            dst_ref=fulls[which].at[there, pl.ds(part * side + piece * cut, piece)],
            send_sem=blk_send.at[which, q, way, cut],
            recv_sem=blk_recv.at[which, there, side, cut],
            device_id={"chi": target},
            device_id_type=MESH,
        )

    def ways(which, q, cut):
        targets = (me + 4, me - 4, me + 2 - 4 * y, sibling)

        def send(way):
            block_copy(which, q, core, way, targets[way], cut).start()

        def leave(way):
            block_copy(which, q, core, way, targets[way], cut).wait_send()

        return send, leave

    def arrived(which, q, side, cut):
        block_copy(which, q, side, SIBLING, sibling, cut).wait_recv()

    def whole(which, lo, hi):
        def wait(slot):
            for cut in range(CUTS):
                here = fulls[which].at[slot, pl.ds(part * (1 - core) + piece * cut, piece)]
                pltpu.make_async_remote_copy(
                    src_ref=here, dst_ref=here, send_sem=blk_send.at[which, 0, SIBLING, cut],
                    recv_sem=blk_recv.at[which, slot, 1 - core, cut],
                    device_id={"chi": sibling}, device_id_type=MESH,
                ).wait_recv()

        each(lo, hi, wait)

    def up_copy(j):
        to = lax.rem(me + j, n)
        return pltpu.make_async_remote_copy(
            src_ref=up_tx.at[to],
            dst_ref=up_rx.at[me],
            send_sem=up_send.at[j],
            recv_sem=up_recv.at[j],
            device_id={"chi": to},
            device_id_type=MESH,
        )

    def each(lo, hi, act):
        def body(j, carry):
            act(j)
            return carry

        lax.fori_loop(lo, hi, body, 0)

    def join(which):
        swap_copy(which).wait_recv()

        def body(j):
            own = ins[which][part * core + j].astype(F32)
            other = swap[which, j].astype(F32)
            first = jnp.where(core == 0, own, other)
            second = jnp.where(core == 0, other, own)
            both = jnp.concatenate([first, second], axis=0)
            if which == LOWER:
                keep = chip_ref[...] + bond_ref[part * core + j] == new_ref[...]
                both = jnp.where(keep, both, jnp.zeros_like(both))
            fulls[which][0, part * core + j] = both.astype(BF)

        each(0, part, body)

    beyond = chip + 1 - 2 * y

    def open_across(which):
        for cut in range(CUTS):
            send, _ = ways(which, chip, cut)
            send(ACROSS)
            send(SIBLING)

    def open_line(which):
        for cut in range(CUTS):
            send, _ = ways(which, chip, cut)
            pl.when(z < depth - 1)(lambda: send(RIGHT))
            pl.when(z > 0)(lambda: send(LEFT))

    def along(which, s):
        for cut in range(CUTS):
            @pl.when(z - s >= 0)
            def _():
                q = chip - 2 * s
                arrived(which, q, core, cut)
                send, _ = ways(which, q, cut)
                pl.when(z < depth - 1)(lambda: send(RIGHT))
                send(ACROSS)
                send(SIBLING)

            @pl.when(z + s < depth)
            def _():
                q = chip + 2 * s
                arrived(which, q, core, cut)
                send, _ = ways(which, q, cut)
                pl.when(z > 0)(lambda: send(LEFT))
                send(ACROSS)
                send(SIBLING)

    def beside(which, s):
        for cut in range(CUTS):
            for sign in (-1, 1) if s else (1,):
                @pl.when(jnp.logical_and(z + sign * s >= 0, z + sign * s < depth))
                def _():
                    q = beyond + 2 * sign * s
                    arrived(which, q, core, cut)
                    block_copy(which, q, core, SIBLING, sibling, cut).start()

    def sent(which):
        def body(q):
            column = q // 2
            mine = lax.rem(q, 2) == y
            for cut in range(CUTS):
                _, leave = ways(which, q, cut)
                pl.when(jnp.logical_and(mine, jnp.logical_and(column <= z, z < depth - 1)))(lambda: leave(RIGHT))
                pl.when(jnp.logical_and(mine, jnp.logical_and(column >= z, z > 0)))(lambda: leave(LEFT))
                pl.when(mine)(lambda: leave(ACROSS))
                leave(SIBLING)

        each(0, chips, body)

    def rows_of(full, t, j):
        lo, hi = LANES * t, LANES * (t + 1)
        cuts = []
        for slot in range(lo // wide, (hi + wide - 1) // wide):
            start, stop = max(lo - slot * wide, 0), min(hi - slot * wide, wide)
            cuts.append(full[slot, j, start:stop, :])
        return cuts

    def first(t, lo, hi):
        def body(j):
            right = jnp.concatenate(rows_of(edge_all, t, 2 * j) + rows_of(edge_all, t, 2 * j + 1), axis=0)
            half = lax.dot_general(up_t[...], right, (((1,), (1,)), ((), ())), preferred_element_type=F32)
            half = half.astype(BF)
            at = pl.multiple_of(2 * j * kdim, 2 * kdim)
            state[t, 1:rows + 1, pl.ds(at, kdim), :] = half[:, :LANES].reshape(rows, kdim, LANES)
            state[t, 1:rows + 1, pl.ds(at + kdim, kdim), :] = half[:, LANES:].reshape(rows, kdim, LANES)

        each(lo, hi, body)

    def second(t, lo, hi):
        def body(j):
            c = GROUP * j
            right = jnp.concatenate([state[t, c + 1 + i] for i in range(GROUP)], axis=1)
            grown = jnp.dot(block_ref[...], right, preferred_element_type=F32).astype(BF)
            for i in range(GROUP):
                state[t, c + i] = grown[:, i * LANES:(i + 1) * LANES]

        each(lo, hi, body)

    def third(t):
        def body(j):
            lefts, rights = [], []
            for i in range(4):
                at = pl.multiple_of((4 * j + i) * kdim, kdim)
                lefts.append(state[t, 0:rows, pl.ds(at, kdim), :].reshape(rows * kdim, LANES))
                rights += rows_of(lower_all, t, 4 * j + i)
            total[...] += jnp.dot(
                jnp.concatenate(lefts, axis=1), jnp.concatenate(rights, axis=0), preferred_element_type=F32
            )

        each(0, kdim // 4, body)

    steps = rows // GROUP
    swap_copy(EDGE).start()
    swap_copy(LOWER).start()
    join(EDGE)
    open_line(EDGE)
    open_across(EDGE)
    upper = jnp.where(own_ref[...] == new_ref[...], upper_ref[...].astype(F32), 0.0).T
    for j in range(n):
        up_tx[j] = upper[j * rows:(j + 1) * rows, :].astype(BF)
    each(1, n, lambda j: up_copy(j).start())
    join(LOWER)
    up_rx[me] = up_tx[me]
    total[...] = jnp.zeros_like(total)
    beside(EDGE, 0)
    along(EDGE, 1)
    for i in range(pairs // LANES):
        turned[i] = site_ref[i * LANES:(i + 1) * LANES, :].astype(F32).T
    for d in range(kdim):
        keep = column_ref[...] + bond_ref[d] == pair_ref[...]
        block_ref[d * kdim:(d + 1) * kdim, :] = jnp.where(
            keep,
            jnp.concatenate(
                [turned[i, pl.ds(d, kdim, stride=kdim), :] for i in range(pairs // LANES)], axis=1
            ),
            0.0,
        ).astype(BF)
    each(1, n, lambda j: up_copy(j).wait_recv())
    up_wide[...] = up_rx[...].astype(F32)
    lane = lax.broadcasted_iota(jnp.int32, (n, width), 1)
    sender = lax.broadcasted_iota(jnp.int32, (n, width), 0)
    spread = jnp.logical_and(lane >= sender * rows, lane < (sender + 1) * rows).astype(F32).astype(BF)
    within = lax.rem(lax.broadcasted_iota(jnp.int32, (rows, 1, width), 2), rows)
    chosen = within == lax.broadcasted_iota(jnp.int32, (rows, 1, width), 0)
    for c in range(rows):
        spots = lax.dot_general(
            up_wide[:, c, :].astype(BF), spread, (((0,), (0,)), ((), ())), preferred_element_type=F32
        ).reshape(rows, kdim, width)
        up_t[c * kdim:(c + 1) * kdim, :] = jnp.sum(jnp.where(chosen, spots, 0.0), axis=0).astype(BF)
    beside(EDGE, 1)
    along(EDGE, 2)
    whole(EDGE, 0, 3)
    first(0, 0, kdim // 2)
    beside(EDGE, 2)
    along(EDGE, 3)
    open_line(LOWER)
    open_across(LOWER)
    second(0, 0, steps)
    beside(EDGE, 3)
    whole(EDGE, 3, 6)
    first(1, 0, kdim // 2)
    beside(LOWER, 0)
    along(LOWER, 1)
    whole(EDGE, 6, chips)
    first(2, 0, kdim // 2)
    second(1, 0, steps // 2)
    beside(LOWER, 1)
    along(LOWER, 2)
    second(1, steps // 2, steps)
    second(2, 0, steps // 2)
    beside(LOWER, 2)
    along(LOWER, 3)
    second(2, steps // 2, steps)
    whole(LOWER, 0, 3)
    third(0)
    whole(LOWER, 3, 6)
    third(1)
    beside(LOWER, 3)
    whole(LOWER, 6, chips)
    third(2)

    peaks[me] = jnp.full(peaks.shape[1:], jnp.max(jnp.abs(total[...])), F32)

    def peak_copy(j):
        return pltpu.make_async_remote_copy(
            src_ref=peaks.at[me],
            dst_ref=peaks.at[me],
            send_sem=peak_send.at[j],
            recv_sem=peak_recv.at[j],
            device_id={"chi": lax.rem(me + j, n)},
            device_id_type=MESH,
        )

    each(1, n, lambda j: peak_copy(j).start())
    each(0, 2, lambda w: pltpu.make_async_remote_copy(
        src_ref=edge_ref.at[pl.ds(0, part)], dst_ref=swap.at[w], send_sem=swap_send.at[w],
        recv_sem=swap_recv.at[w], device_id={"chi": sibling}, device_id_type=MESH).wait_send())
    each(1, n, lambda j: up_copy(j).wait_send())
    sent(EDGE)
    sent(LOWER)
    each(1, n, lambda j: peak_copy(j).wait_recv())
    each(1, n, lambda j: peak_copy(j).wait_send())
    largest = jnp.max(peaks[...])
    out_ref[...] = (total[...] / (largest + 1e-06)).astype(BF)


def fused(n, edge, proj_upper, proj_lower, site, chi_charge, bond_charge, new_charge):
    rows, kdim, width = edge.shape
    mine = lax.axis_index("chi") * rows
    own = lax.dynamic_slice_in_dim(chi_charge, mine, rows)
    own = (own[:, None] + bond_charge[None, :]).reshape(rows * kdim, 1)
    start = lax.axis_index("chi") // 2 * (2 * rows)
    chip = lax.dynamic_slice_in_dim(chi_charge, start, 2 * rows)[:, None]
    pair = (bond_charge[:, None] + bond_charge[None, :]).reshape(kdim * kdim)
    chips = n // 2
    part = kdim // 2
    dma = pltpu.SemaphoreType.DMA
    vmem = pl.BlockSpec(memory_space=pltpu.VMEM)
    out = pl.pallas_call(
        functools.partial(kernel, n, chips // 2),
        out_shape=jax.ShapeDtypeStruct((rows * kdim, width), BF),
        in_specs=[vmem] * 9 + [pl.BlockSpec(memory_space=pltpu.SMEM)],
        out_specs=vmem,
        scratch_shapes=[
            pltpu.VMEM((chips, kdim, 2 * rows, width), BF),
            pltpu.VMEM((chips, kdim, 2 * rows, width), BF),
            pltpu.VMEM((2, part, rows, width), BF),
            pltpu.VMEM((n, rows, rows * kdim), BF),
            pltpu.VMEM((n, rows, rows * kdim), BF),
            pltpu.VMEM((n, rows, rows * kdim), F32),
            pltpu.VMEM((rows * kdim, width), BF),
            pltpu.VMEM((kdim * kdim // LANES, kdim * kdim, LANES), F32),
            pltpu.VMEM((kdim * kdim, kdim * kdim), BF),
            pltpu.VMEM((width // LANES, rows + 1, kdim * kdim, LANES), BF),
            pltpu.VMEM((rows * kdim, width), F32),
            pltpu.VMEM((n, 8, 128), F32),
            dma((2,)), dma((2,)),
            dma((n,)), dma((n,)),
            dma((2, chips, 4, CUTS)), dma((2, chips, 2, CUTS)),
            dma((n,)), dma((n,)),
        ],
        compiler_params=pltpu.CompilerParams(
            collective_id=0, has_side_effects=True, vmem_limit_bytes=63 * 1024 * 1024
        ),
        name="edge_update",
    )(
        edge.transpose(1, 0, 2), proj_lower.transpose(1, 0, 2), proj_upper.reshape(rows * kdim, width), site,
        own, chip, new_charge[None, :], pair[None, :], bond_charge[:, None], bond_charge,
    )
    return out.reshape(rows, kdim, width)


def solution(mesh):
    n = mesh.shape["chi"]

    def local(edge, *rest):
        rows, kdim, width = edge.shape
        if n == 16 and rows % 8 == 0 and rows % 6 == 0 and kdim % 32 == 0 and width == 3 * LANES:
            return fused(n, edge, *rest)
        return plain(edge, *rest)

    placed = (
        P(("grp", "chi"), None, None),
        P(("grp", "chi"), None, None),
        P(("grp", "chi"), None, None),
        P("grp", None),
        P("grp"),
        P("grp"),
        P("grp"),
    )
    return jax.shard_map(
        local, mesh=mesh, in_specs=placed, out_specs=P(("grp", "chi"), None, None), check_vma=False
    )
```
